32 devices in a mesh: aux: 8 (over z, x), grp: 4 (over y, core).
Axes of the slice: x: 2, y: 2, z: 4, core: 2. Of those that a mesh axis runs over, the one named last changes fastest.
Arguments:
- occ_blocks: bfloat16 [32, 128, 256], P('aux'), may hold values from -6 to 6
- virt_blocks: bfloat16 [32, 128, 256], P('aux'), may hold values from -6 to 6
- three_center: bfloat16 [16384, 1024], P(('aux', 'grp')), may hold values from -0.1875 to 0.1875
- blk_index: int32 [8, 8], P(None, 'aux'), may hold values from 0 to 3
- blk_live: int32 [8, 8], P(None, 'aux'), may hold values 0 or 1
- live_counts: int32 [16], replicated, may hold values from 1 to 16
Outputs:
- polarizability: float32 [16384, 2048], P(('aux', 'grp'))
The draws below stay inside these ranges and needn't reach their ends.
All inputs are finite; a program needn't handle non-finite values. No bound on the sum of `blk_live` on one device may be relied on, other than what follows from the above.
Results may differ from the reference program's by a relative error of at most 0.0041.
Values may be sent and summed in bfloat16 or wider, within the bound.
A program may use at most 128 MiB of HBM per device.

```python
import math
import jax
import jax.numpy as jnp
from jax import lax

AUX_DEV = 512
BS = 128
WIN = 256
GB_DEV = 4
NBLK = 32
AUX = 16384
SLOTS = 1024
N_AUX = 8
N_GRP = 4


def set_ends(result, key, smallest, top_value):
    longest = result.shape.index(max(result.shape))
    spots = []
    for shift in (0, 1):
        where = [jax.random.randint(jax.random.fold_in(key, axis), (), 0, length) for axis, length in enumerate(result.shape)]
        where[longest] = (where[longest] + shift) % result.shape[longest]
        spots.append(tuple(where))
    return result.at[spots[0]].set(smallest).at[spots[1]].set(top_value)


def block_scale(key, dims, split, smallest, top_value):
    def one(position, blocks):
        steps = jax.random.uniform(jax.random.fold_in(jax.random.fold_in(key, 6), position), (blocks,), jnp.float32, smallest / len(split), top_value / len(split))
        return jnp.repeat(jnp.exp(steps), dims[position] // blocks).reshape((-1,) + (1,) * (len(dims) - position - 1))

    gain = one(*split[0])
    for cut in split[1:]:
        gain = gain * one(*cut)
    return gain


def normal_values(stream_key, shape, deviation, most, split=(), held_as=jnp.bfloat16):
    gain = block_scale(stream_key, shape, split, -0.22, 0.18) if split else 1.0
    drawn = jax.random.normal(stream_key, shape, jnp.float32) * deviation * gain
    return jnp.minimum(jnp.maximum(drawn, -most), most).astype(held_as)


def setup_inputs(seed: int = 0) -> dict:
    key_of = jax.random.split(jax.random.key(seed), 7)
    return {
        "occ_blocks": normal_values(key_of[0], (NBLK, BS, WIN), 1.0, 6.0, ((0, 8),)),
        "virt_blocks": normal_values(key_of[1], (NBLK, BS, WIN), 1.0, 6.0, ((0, 8),)),
        "three_center": normal_values(key_of[2], (AUX, SLOTS), SLOTS ** -0.5, 0.1875, ((0, 32),)),
        "blk_index": set_ends(jax.random.randint(key_of[3], (N_AUX, N_AUX), 0, GB_DEV), jax.random.fold_in(key_of[3], 1), 0, GB_DEV - 1).astype(jnp.int32),
        "blk_live": set_ends((jax.random.randint(key_of[4], (N_AUX, N_AUX), 0, 2) < 1).astype(jnp.int32), jax.random.fold_in(key_of[4], 1), 0, 1),
        "live_counts": set_ends(jax.random.randint(key_of[5], (WIN // 16,), 1, 17), jax.random.fold_in(key_of[5], 1), 1, 16).astype(jnp.int32),
    }


group_width = 16

def reference(occ_blocks, virt_blocks, three_center, blk_index, blk_live, live_counts):
    group = AUX_DEV * N_GRP
    columns = jnp.arange(WIN, dtype=jnp.int32)
    limits = live_counts[columns // group_width]
    col_mask = (columns % group_width < limits).astype(jnp.float32)
    scale = 1.0 / math.sqrt(WIN)

    def one_tile(owner):
        holders = jnp.arange(N_AUX, dtype=jnp.int32) * GB_DEV + blk_index[owner].astype(jnp.int32)
        keep = blk_live[owner].astype(jnp.bfloat16)[:, None, None]
        stack_occ = (occ_blocks[holders] * keep).reshape(N_AUX * BS, WIN)
        stack_virt = (virt_blocks[holders] * keep).reshape(N_AUX * BS, WIN)
        tiles = lax.dynamic_slice_in_dim(three_center, owner * group, group, 0)
        half_occ = (jnp.dot(tiles, stack_occ, preferred_element_type=jnp.float32) * col_mask).astype(jnp.bfloat16)
        half_virt = jnp.dot(tiles, stack_virt, preferred_element_type=jnp.float32).astype(jnp.bfloat16)
        pairs = lax.dot_general(half_occ, half_virt, (((1,), (1,)), ((), ())), preferred_element_type=jnp.float32)
        return pairs * scale
    blocks_out = lax.map(one_tile, jnp.arange(N_AUX, dtype=jnp.int32))
    return blocks_out.reshape(N_AUX * group, group)
```

```python
import functools
import math

import jax
import jax.numpy as jnp
from jax import lax
from jax.experimental import pallas as pl
from jax.experimental.pallas import tpu as pltpu
from jax.sharding import PartitionSpec as P

group_width = 16
MESH = pl.DeviceIdType.MESH
chunks = 4
depth = 1024


def route(
    n, idx_ref, live_ref, counts_ref, occ_ref, virt_ref, tc_hbm,
    half_occ, half_virt,
    send, stack, tc, load_sem, send_sem, recv_sem, pass_sem, got_sem, gs_sem, gr_sem,
):
    me = lax.axis_index("aux")
    g = lax.axis_index("grp")
    row, core = g // 2, g % 2
    twin = row * 2 + (1 - core)
    across = (1 - row) * 2 + core
    opposite = (1 - row) * 2 + (1 - core)
    size = virt_ref.shape[1]
    part = size // 2
    rows = tc.shape[0]
    step = rows // chunks

    load = pltpu.make_async_copy(tc_hbm, tc, load_sem.at[0])
    load.start()

    barrier = pltpu.get_barrier_semaphore()

    @pl.loop(1, n)
    def _(k):
        pl.semaphore_signal(
            barrier, inc=1, device_id={"aux": lax.rem(me + k, n)}, device_id_type=MESH
        )

    for peer in (twin, across):
        pl.semaphore_signal(barrier, inc=1, device_id={"grp": peer}, device_id_type=MESH)

    mine = pl.multiple_of(core * part, part)

    def stage(a):
        blocks = (virt_ref, occ_ref)[a]

        @pl.loop(1, n)
        def _(k):
            t = lax.rem(me + k, n)
            keep = live_ref[t, 0].astype(jnp.float32)
            piece = blocks[idx_ref[t, 0], pl.ds(mine, part), :]
            send[a, t] = (piece.astype(jnp.float32) * keep).astype(jnp.bfloat16)

        keep = live_ref[me, 0].astype(jnp.float32)
        own = blocks[idx_ref[me, 0]]
        stack[a, pl.ds(pl.multiple_of(me * size, size), size), :] = (
            own.astype(jnp.float32) * keep
        ).astype(jnp.bfloat16)

    def out_copy(a, t):
        here = pl.ds(pl.multiple_of(me * size + core * part, part), part)
        return pltpu.make_async_remote_copy(
            send.at[a, t], stack.at[a, here, :], send_sem.at[a, t], recv_sem.at[a, me],
            device_id={"aux": t}, device_id_type=MESH,
        )

    def in_copy(a, s):
        there = pl.ds(pl.multiple_of(s * size + core * part, part), part)
        return pltpu.make_async_remote_copy(
            send.at[a, s], stack.at[a, there, :], send_sem.at[a, s], recv_sem.at[a, s],
            device_id={"aux": s}, device_id_type=MESH,
        )

    def pass_copy(a, s, side):
        spot = pl.ds(pl.multiple_of(s * size + side * part, part), part)
        return pltpu.make_async_remote_copy(
            stack.at[a, spot, :], stack.at[a, spot, :], pass_sem.at[a, s], got_sem.at[a, s],
            device_id={"grp": twin}, device_id_type=MESH,
        )

    def start_all(a):
        @pl.loop(1, n)
        def _(k):
            out_copy(a, lax.rem(me + k, n)).start()

    def sent_all(a):
        @pl.loop(1, n)
        def _(k):
            out_copy(a, lax.rem(me + k, n)).wait_send()

    def pass_all(a):
        @pl.loop(1, n)
        def _(k):
            s = lax.rem(me + n - k, n)
            in_copy(a, s).wait_recv()
            pass_copy(a, s, core).start()

    def got_all(a):
        @pl.loop(1, n)
        def _(k):
            s = lax.rem(me + n - k, n)
            pass_copy(a, s, 1 - core).wait_recv()
            pass_copy(a, s, core).wait_send()

    def product(a, first):
        wide = tc.shape[1]
        deep = min(depth, wide)

        def term(i, total):
            at = pl.ds(pl.multiple_of(i * deep, deep), deep)
            return total + jnp.dot(
                tc[first : first + step, at], stack[a, at, :], preferred_element_type=jnp.float32
            )

        if wide == deep:
            return jnp.dot(
                tc[first : first + step, :], stack[a], preferred_element_type=jnp.float32
            )
        return lax.fori_loop(
            0, wide // deep, term, jnp.zeros((step, stack.shape[2]), jnp.float32)
        )

    def gather_copy(kind, origin, j, peer):
        spot = pl.ds(pl.multiple_of(origin * rows + j * step, step), step)
        return pltpu.make_async_remote_copy(
            half_virt.at[spot, :], half_virt.at[spot, :], gs_sem.at[kind, j], gr_sem.at[kind, j],
            device_id={"grp": peer}, device_id_type=MESH,
        )

    stage(0)
    pl.semaphore_wait(barrier, n + 1)
    start_all(0)
    stage(1)
    sent_all(0)
    start_all(1)
    pass_all(0)
    load.wait()
    got_all(0)
    for j in range(chunks):
        spot = pl.ds(pl.multiple_of(g * rows + j * step, step), step)
        half_virt[spot, :] = product(0, j * step).astype(jnp.bfloat16)
        gather_copy(0, g, j, across).start()
        gather_copy(1, g, j, twin).start()
    pass_all(1)
    for j in range(chunks):
        gather_copy(0, across, j, across).wait_recv()
        gather_copy(2, across, j, twin).start()
    got_all(1)

    column = lax.broadcasted_iota(jnp.int32, (1, stack.shape[2]), 1)
    owner = column // group_width
    limit = jnp.zeros_like(column)
    for q in range(counts_ref.shape[0]):
        limit = jnp.where(owner == q, counts_ref[q], limit)
    mask = jnp.where(column - owner * group_width < limit, 1.0, 0.0).astype(jnp.float32)
    for j in range(chunks):
        half_occ[j * step : (j + 1) * step, :] = (product(1, j * step) * mask).astype(jnp.bfloat16)

    sent_all(1)
    for j in range(chunks):
        gather_copy(0, g, j, across).wait_send()
        gather_copy(1, g, j, twin).wait_send()
        gather_copy(1, twin, j, twin).wait_recv()
        gather_copy(2, across, j, twin).wait_send()
        gather_copy(2, opposite, j, twin).wait_recv()


def body(occ_blocks, virt_blocks, three_center, blk_index, blk_live, live_counts):
    n = lax.axis_size("aux")
    parts = lax.axis_size("grp")
    _, size, width = occ_blocks.shape
    rows, slots = three_center.shape
    scale = 1.0 / math.sqrt(width)
    smem = pl.BlockSpec(memory_space=pltpu.SMEM)
    hbm = pl.BlockSpec(memory_space=pl.ANY)
    vmem = pl.BlockSpec(memory_space=pltpu.VMEM)
    dma = pltpu.SemaphoreType.DMA
    half_occ, half_virt = pl.pallas_call(
        functools.partial(route, n),
        out_shape=(
            jax.ShapeDtypeStruct((rows, width), jnp.bfloat16),
            jax.ShapeDtypeStruct((parts * rows, width), jnp.bfloat16),
        ),
        in_specs=[smem, smem, smem, vmem, vmem, hbm],
        out_specs=(vmem, vmem),
        scratch_shapes=[
            pltpu.VMEM((2, n, size // 2, width), jnp.bfloat16),
            pltpu.VMEM((2, n * size, width), jnp.bfloat16),
            pltpu.VMEM((rows, slots), jnp.bfloat16),
            dma((1,)),
            dma((2, n)), dma((2, n)), dma((2, n)), dma((2, n)),
            dma((3, chunks)), dma((3, chunks)),
        ],
        compiler_params=pltpu.CompilerParams(
            collective_id=0, has_side_effects=True, vmem_limit_bytes=48 * 1024 * 1024
        ),
        cost_estimate=pl.CostEstimate(
            flops=4 * rows * slots * width, bytes_accessed=2 * rows * slots, transcendentals=0
        ),
    )(blk_index, blk_live, live_counts, occ_blocks, virt_blocks, three_center)
    return (
        lax.dot_general(
            half_occ, half_virt, (((1,), (1,)), ((), ())), preferred_element_type=jnp.float32
        )
        * scale
    )


def solution(mesh):
    placed = (
        P("aux", None, None),
        P("aux", None, None),
        P(("aux", "grp"), None),
        P(None, "aux"),
        P(None, "aux"),
        P(),
    )
    return jax.shard_map(
        body, mesh=mesh, in_specs=placed, out_specs=P(("aux", "grp"), None), check_vma=False
    )
```

```python
import functools
import math

import jax
import jax.numpy as jnp
from jax import lax
from jax.experimental import pallas as pl
from jax.experimental.pallas import tpu as pltpu
from jax.sharding import PartitionSpec as P

group_width = 16
MESH = pl.DeviceIdType.MESH
chunks = 4
depth = 1024


def route(
    n, idx_hbm, live_hbm, counts_hbm, occ_hbm, virt_hbm, tc_hbm,
    half_occ, half_virt,
    idx_ref, live_ref, counts_ref, occ_ref, virt_ref, send, stack, tc, load_sem, send_sem, recv_sem, pass_sem, got_sem, gs_sem, gr_sem,
):
    me = lax.axis_index("aux")
    g = lax.axis_index("grp")
    row, core = g // 2, g % 2
    twin = row * 2 + (1 - core)
    across = (1 - row) * 2 + core
    opposite = (1 - row) * 2 + (1 - core)
    size = virt_ref.shape[1]
    part = size // 2
    rows = tc.shape[0]
    step = rows // chunks

    pairs = (
        (idx_hbm, idx_ref), (live_hbm, live_ref), (counts_hbm, counts_ref),
        (virt_hbm, virt_ref), (occ_hbm, occ_ref), (tc_hbm, tc),
    )
    loads = [
        pltpu.make_async_copy(src, dst, load_sem.at[i]) for i, (src, dst) in enumerate(pairs)
    ]
    for load in loads:
        load.start()

    barrier = pltpu.get_barrier_semaphore()

    @pl.loop(1, n)
    def _(k):
        pl.semaphore_signal(
            barrier, inc=1, device_id={"aux": lax.rem(me + k, n)}, device_id_type=MESH
        )

    for peer in (twin, across):
        pl.semaphore_signal(barrier, inc=1, device_id={"grp": peer}, device_id_type=MESH)

    mine = pl.multiple_of(core * part, part)

    def stage(a):
        blocks = (virt_ref, occ_ref)[a]

        @pl.loop(1, n)
        def _(k):
            t = lax.rem(me + k, n)
            keep = live_ref[0, t].astype(jnp.float32)
            piece = blocks[idx_ref[0, t], pl.ds(mine, part), :]
            send[a, t] = (piece.astype(jnp.float32) * keep).astype(jnp.bfloat16)

        keep = live_ref[0, me].astype(jnp.float32)
        own = blocks[idx_ref[0, me]]
        stack[a, pl.ds(pl.multiple_of(me * size, size), size), :] = (
            own.astype(jnp.float32) * keep
        ).astype(jnp.bfloat16)

    def out_copy(a, t):
        here = pl.ds(pl.multiple_of(me * size + core * part, part), part)
        return pltpu.make_async_remote_copy(
            send.at[a, t], stack.at[a, here, :], send_sem.at[a, t], recv_sem.at[a, me],
            device_id={"aux": t}, device_id_type=MESH,
        )

    def in_copy(a, s):
        there = pl.ds(pl.multiple_of(s * size + core * part, part), part)
        return pltpu.make_async_remote_copy(
            send.at[a, s], stack.at[a, there, :], send_sem.at[a, s], recv_sem.at[a, s],
            device_id={"aux": s}, device_id_type=MESH,
        )

    def pass_copy(a, s, side):
        spot = pl.ds(pl.multiple_of(s * size + side * part, part), part)
        return pltpu.make_async_remote_copy(
            stack.at[a, spot, :], stack.at[a, spot, :], pass_sem.at[a, s], got_sem.at[a, s],
            device_id={"grp": twin}, device_id_type=MESH,
        )

    def start_all(a):
        @pl.loop(1, n)
        def _(k):
            out_copy(a, lax.rem(me + k, n)).start()

    def sent_all(a):
        @pl.loop(1, n)
        def _(k):
            out_copy(a, lax.rem(me + k, n)).wait_send()

    def pass_all(a):
        @pl.loop(1, n)
        def _(k):
            s = lax.rem(me + n - k, n)
            in_copy(a, s).wait_recv()
            pass_copy(a, s, core).start()

    def got_all(a):
        @pl.loop(1, n)
        def _(k):
            s = lax.rem(me + n - k, n)
            pass_copy(a, s, 1 - core).wait_recv()
            pass_copy(a, s, core).wait_send()

    def product(a, first):
        wide = tc.shape[1]
        deep = min(depth, wide)

        def term(i, total):
            at = pl.ds(pl.multiple_of(i * deep, deep), deep)
            return total + jnp.dot(
                tc[first : first + step, at], stack[a, at, :], preferred_element_type=jnp.float32
            )

        if wide == deep:
            return jnp.dot(
                tc[first : first + step, :], stack[a], preferred_element_type=jnp.float32
            )
        return lax.fori_loop(
            0, wide // deep, term, jnp.zeros((step, stack.shape[2]), jnp.float32)
        )

    def gather_copy(kind, origin, j, peer):
        spot = pl.ds(pl.multiple_of(origin * rows + j * step, step), step)
        return pltpu.make_async_remote_copy(
            half_virt.at[spot, :], half_virt.at[spot, :], gs_sem.at[kind, j], gr_sem.at[kind, j],
            device_id={"grp": peer}, device_id_type=MESH,
        )

    for load in loads[:4]:
        load.wait()
    stage(0)
    pl.semaphore_wait(barrier, n + 1)
    start_all(0)
    loads[4].wait()
    stage(1)
    sent_all(0)
    start_all(1)
    pass_all(0)
    loads[5].wait()
    got_all(0)
    for j in range(chunks):
        spot = pl.ds(pl.multiple_of(g * rows + j * step, step), step)
        half_virt[spot, :] = product(0, j * step).astype(jnp.bfloat16)
        gather_copy(0, g, j, across).start()
        gather_copy(1, g, j, twin).start()
    pass_all(1)
    for j in range(chunks):
        gather_copy(0, across, j, across).wait_recv()
        gather_copy(2, across, j, twin).start()
    got_all(1)

    column = lax.broadcasted_iota(jnp.int32, (1, stack.shape[2]), 1)
    owner = column // group_width
    limit = jnp.zeros_like(column)
    for q in range(counts_ref.shape[0]):
        limit = jnp.where(owner == q, counts_ref[q], limit)
    mask = jnp.where(column - owner * group_width < limit, 1.0, 0.0).astype(jnp.float32)
    for j in range(chunks):
        half_occ[j * step : (j + 1) * step, :] = (product(1, j * step) * mask).astype(jnp.bfloat16)

    sent_all(1)
    for j in range(chunks):
        gather_copy(0, g, j, across).wait_send()
        gather_copy(1, g, j, twin).wait_send()
        gather_copy(1, twin, j, twin).wait_recv()
        gather_copy(2, across, j, twin).wait_send()
        gather_copy(2, opposite, j, twin).wait_recv()


def body(occ_blocks, virt_blocks, three_center, blk_index, blk_live, live_counts):
    n = lax.axis_size("aux")
    parts = lax.axis_size("grp")
    local, size, width = occ_blocks.shape
    rows, slots = three_center.shape
    scale = 1.0 / math.sqrt(width)
    hbm = pl.BlockSpec(memory_space=pltpu.HBM)
    vmem = pl.BlockSpec(memory_space=pltpu.VMEM)
    dma = pltpu.SemaphoreType.DMA
    half_occ, half_virt = pl.pallas_call(
        functools.partial(route, n),
        out_shape=(
            jax.ShapeDtypeStruct((rows, width), jnp.bfloat16),
            jax.ShapeDtypeStruct((parts * rows, width), jnp.bfloat16),
        ),
        in_specs=[hbm] * 6,
        out_specs=(vmem, vmem),
        scratch_shapes=[
            pltpu.SMEM((1, n), jnp.int32),
            pltpu.SMEM((1, n), jnp.int32),
            pltpu.SMEM(live_counts.shape, jnp.int32),
            pltpu.VMEM((local, size, width), jnp.bfloat16),
            pltpu.VMEM((local, size, width), jnp.bfloat16),
            pltpu.VMEM((2, n, size // 2, width), jnp.bfloat16),
            pltpu.VMEM((2, n * size, width), jnp.bfloat16),
            pltpu.VMEM((rows, slots), jnp.bfloat16),
            dma((6,)),
            dma((2, n)), dma((2, n)), dma((2, n)), dma((2, n)),
            dma((3, chunks)), dma((3, chunks)),
        ],
        compiler_params=pltpu.CompilerParams(
            collective_id=0, has_side_effects=True, vmem_limit_bytes=48 * 1024 * 1024
        ),
        cost_estimate=pl.CostEstimate(
            flops=4 * rows * slots * width, bytes_accessed=2 * rows * slots, transcendentals=0
        ),
    )(*[
        pltpu.with_memory_space_constraint(x, pltpu.HBM)
        for x in (blk_index.T, blk_live.T, live_counts, occ_blocks, virt_blocks, three_center)
    ])
    return (
        lax.dot_general(
            half_occ, half_virt, (((1,), (1,)), ((), ())), preferred_element_type=jnp.float32
        )
        * scale
    )


def solution(mesh):
    placed = (
        P("aux", None, None),
        P("aux", None, None),
        P(("aux", "grp"), None),
        P(None, "aux"),
        P(None, "aux"),
        P(),
    )
    return jax.shard_map(
        body, mesh=mesh, in_specs=placed, out_specs=P(("aux", "grp"), None), check_vma=False
    )
```

```python
import functools
import math

import jax
import jax.numpy as jnp
from jax import lax
from jax.experimental import pallas as pl
from jax.experimental.pallas import tpu as pltpu
from jax.sharding import PartitionSpec as P

group_width = 16
MESH = pl.DeviceIdType.MESH
chunks = 2
depth = 1024


def route(
    n, idx_hbm, live_hbm, counts_hbm, occ_hbm, virt_hbm, tc_hbm,
    half_occ, half_virt,
    idx_ref, live_ref, counts_ref, occ_ref, virt_ref, send_a, send_b, send_c, stack_a, stack_b, stack_c, tc, load_sem, send_sem, recv_sem, pass_sem, got_sem, gs_sem, gr_sem,
):
    sends, stacks = (send_a, send_b, send_c), (stack_a, stack_b, stack_c)
    half = stack_a.shape[1]
    me = lax.axis_index("aux")
    g = lax.axis_index("grp")
    row, core = g // 2, g % 2
    twin = row * 2 + (1 - core)
    across = (1 - row) * 2 + core
    opposite = (1 - row) * 2 + (1 - core)
    size = virt_ref.shape[1]
    part = size // 2
    rows = tc.shape[0]
    step = rows // chunks

    pairs = (
        (idx_hbm, idx_ref), (live_hbm, live_ref), (counts_hbm, counts_ref),
        (virt_hbm, virt_ref), (occ_hbm, occ_ref), (tc_hbm, tc),
    )
    loads = [
        pltpu.make_async_copy(src, dst, load_sem.at[i]) for i, (src, dst) in enumerate(pairs)
    ]
    for load in loads:
        load.start()

    barrier = pltpu.get_barrier_semaphore()

    @pl.loop(1, n)
    def _(k):
        pl.semaphore_signal(
            barrier, inc=1, device_id={"aux": lax.rem(me + k, n)}, device_id_type=MESH
        )

    for peer in (twin, across):
        pl.semaphore_signal(barrier, inc=1, device_id={"grp": peer}, device_id_type=MESH)

    mine = pl.multiple_of(core * part, part)

    def stage(a):
        blocks = (virt_ref, virt_ref, occ_ref)[a]
        cols = (slice(0, half), slice(half, 2 * half), slice(None))[a]
        send, stack = sends[a], stacks[a]

        @pl.loop(1, n)
        def _(k):
            t = lax.rem(me + k, n)
            keep = live_ref[0, t].astype(jnp.float32)
            piece = blocks[idx_ref[0, t], pl.ds(mine, part), cols]
            send[t] = (piece.astype(jnp.float32) * keep).astype(jnp.bfloat16)

        keep = live_ref[0, me].astype(jnp.float32)
        own = blocks[idx_ref[0, me], :, cols]
        stack[pl.ds(pl.multiple_of(me * size, size), size), :] = (
            own.astype(jnp.float32) * keep
        ).astype(jnp.bfloat16)

    def out_copy(a, t):
        here = pl.ds(pl.multiple_of(me * size + core * part, part), part)
        return pltpu.make_async_remote_copy(
            sends[a].at[t], stacks[a].at[here, :], send_sem.at[a, t], recv_sem.at[a, me],
            device_id={"aux": t}, device_id_type=MESH,
        )

    def in_copy(a, s):
        there = pl.ds(pl.multiple_of(s * size + core * part, part), part)
        return pltpu.make_async_remote_copy(
            sends[a].at[s], stacks[a].at[there, :], send_sem.at[a, s], recv_sem.at[a, s],
            device_id={"aux": s}, device_id_type=MESH,
        )

    def pass_copy(a, s, side):
        spot = pl.ds(pl.multiple_of(s * size + side * part, part), part)
        return pltpu.make_async_remote_copy(
            stacks[a].at[spot, :], stacks[a].at[spot, :], pass_sem.at[a, s], got_sem.at[a, s],
            device_id={"grp": twin}, device_id_type=MESH,
        )

    def start_all(a):
        @pl.loop(1, n)
        def _(k):
            out_copy(a, lax.rem(me + k, n)).start()

    def sent_all(a):
        @pl.loop(1, n)
        def _(k):
            out_copy(a, lax.rem(me + k, n)).wait_send()

    def pass_all(a):
        @pl.loop(1, n)
        def _(k):
            s = lax.rem(me + n - k, n)
            in_copy(a, s).wait_recv()
            pass_copy(a, s, core).start()

    def got_all(a):
        @pl.loop(1, n)
        def _(k):
            s = lax.rem(me + n - k, n)
            pass_copy(a, s, 1 - core).wait_recv()
            pass_copy(a, s, core).wait_send()

    def product(a, first):
        stack = stacks[a]
        wide = tc.shape[1]
        deep = min(depth, wide)

        def term(i, total):
            at = pl.ds(pl.multiple_of(i * deep, deep), deep)
            return total + jnp.dot(
                tc[first : first + step, at], stack[at, :], preferred_element_type=jnp.float32
            )

        if wide == deep:
            return jnp.dot(
                tc[first : first + step, :], stack[...], preferred_element_type=jnp.float32
            )
        return lax.fori_loop(
            0, wide // deep, term, jnp.zeros((step, stack.shape[1]), jnp.float32)
        )

    def gather_copy(kind, origin, h, j, peer):
        cols = slice(h * half, (h + 1) * half)
        lane = h * chunks + j
        spot = pl.ds(pl.multiple_of(origin * rows + j * step, step), step)
        return pltpu.make_async_remote_copy(
            half_virt.at[spot, cols], half_virt.at[spot, cols], gs_sem.at[kind, lane], gr_sem.at[kind, lane],
            device_id={"grp": peer}, device_id_type=MESH,
        )

    for load in loads[:4]:
        load.wait()
    def half_product(h):
        for j in range(chunks):
            spot = pl.ds(pl.multiple_of(g * rows + j * step, step), step)
            half_virt[spot, h * half : (h + 1) * half] = product(h, j * step).astype(jnp.bfloat16)
            gather_copy(0, g, h, j, across).start()
            gather_copy(1, g, h, j, twin).start()

    def relay(h):
        for j in range(chunks):
            gather_copy(0, across, h, j, across).wait_recv()
            gather_copy(2, across, h, j, twin).start()

    stage(0)
    pl.semaphore_wait(barrier, n + 1)
    start_all(0)
    stage(1)
    loads[4].wait()
    stage(2)
    sent_all(0)
    start_all(1)
    pass_all(0)
    loads[5].wait()
    got_all(0)
    half_product(0)
    sent_all(1)
    start_all(2)
    pass_all(1)
    got_all(1)
    half_product(1)
    relay(0)
    relay(1)
    pass_all(2)
    got_all(2)

    column = lax.broadcasted_iota(jnp.int32, (1, 2 * half), 1)
    owner = column // group_width
    limit = jnp.zeros_like(column)
    for q in range(counts_ref.shape[0]):
        limit = jnp.where(owner == q, counts_ref[q], limit)
    mask = jnp.where(column - owner * group_width < limit, 1.0, 0.0).astype(jnp.float32)
    for j in range(chunks):
        half_occ[j * step : (j + 1) * step, :] = (product(2, j * step) * mask).astype(jnp.bfloat16)

    sent_all(2)
    for h in range(2):
        for j in range(chunks):
            gather_copy(0, g, h, j, across).wait_send()
            gather_copy(1, g, h, j, twin).wait_send()
            gather_copy(1, twin, h, j, twin).wait_recv()
            gather_copy(2, across, h, j, twin).wait_send()
            gather_copy(2, opposite, h, j, twin).wait_recv()


def body(occ_blocks, virt_blocks, three_center, blk_index, blk_live, live_counts):
    n = lax.axis_size("aux")
    parts = lax.axis_size("grp")
    local, size, width = occ_blocks.shape
    rows, slots = three_center.shape
    widths = (width // 2, width // 2, width)
    scale = 1.0 / math.sqrt(width)
    hbm = pl.BlockSpec(memory_space=pltpu.HBM)
    vmem = pl.BlockSpec(memory_space=pltpu.VMEM)
    dma = pltpu.SemaphoreType.DMA
    half_occ, half_virt = pl.pallas_call(
        functools.partial(route, n),
        out_shape=(
            jax.ShapeDtypeStruct((rows, width), jnp.bfloat16),
            jax.ShapeDtypeStruct((parts * rows, width), jnp.bfloat16),
        ),
        in_specs=[hbm] * 6,
        out_specs=(vmem, vmem),
        scratch_shapes=[
            pltpu.SMEM((1, n), jnp.int32),
            pltpu.SMEM((1, n), jnp.int32),
            pltpu.SMEM(live_counts.shape, jnp.int32),
            pltpu.VMEM((local, size, width), jnp.bfloat16),
            pltpu.VMEM((local, size, width), jnp.bfloat16),
            *[pltpu.VMEM((n, size // 2, w), jnp.bfloat16) for w in widths],
            *[pltpu.VMEM((n * size, w), jnp.bfloat16) for w in widths],
            pltpu.VMEM((rows, slots), jnp.bfloat16),
            dma((6,)),
            dma((3, n)), dma((3, n)), dma((3, n)), dma((3, n)),
            dma((3, 2 * chunks)), dma((3, 2 * chunks)),
        ],
        compiler_params=pltpu.CompilerParams(
            collective_id=0, has_side_effects=True, vmem_limit_bytes=48 * 1024 * 1024
        ),
        cost_estimate=pl.CostEstimate(
            flops=4 * rows * slots * width, bytes_accessed=2 * rows * slots, transcendentals=0
        ),
    )(*[
        pltpu.with_memory_space_constraint(x, pltpu.HBM)
        for x in (blk_index.T, blk_live.T, live_counts, occ_blocks, virt_blocks, three_center)
    ])
    return (
        lax.dot_general(
            half_occ, half_virt, (((1,), (1,)), ((), ())), preferred_element_type=jnp.float32
        )
        * scale
    )


def solution(mesh):
    placed = (
        P("aux", None, None),
        P("aux", None, None),
        P(("aux", "grp"), None),
        P(None, "aux"),
        P(None, "aux"),
        P(),
    )
    return jax.shard_map(
        body, mesh=mesh, in_specs=placed, out_specs=P(("aux", "grp"), None), check_vma=False
    )
```

```python
import functools
import math

import jax
import jax.numpy as jnp
from jax import lax
from jax.experimental import pallas as pl
from jax.experimental.pallas import tpu as pltpu
from jax.sharding import PartitionSpec as P

group_width = 16
MESH = pl.DeviceIdType.MESH
chunks = 1
depth = 1024


def route(
    n, idx_hbm, live_hbm, counts_hbm, occ_hbm, virt_hbm, tc_hbm,
    half_occ, half_virt,
    idx_ref, live_ref, counts_ref, occ_ref, virt_ref, send_a, send_b, send_c, stack_a, stack_b, stack_c, tc, load_sem, send_sem, recv_sem, pass_sem, got_sem, gs_sem, gr_sem,
):
    sends, stacks = (send_a, send_b, send_c), (stack_a, stack_b, stack_c)
    half = stack_a.shape[1]
    me = lax.axis_index("aux")
    g = lax.axis_index("grp")
    row, core = g // 2, g % 2
    twin = row * 2 + (1 - core)
    across = (1 - row) * 2 + core
    opposite = (1 - row) * 2 + (1 - core)
    size = virt_ref.shape[1]
    part = size // 2
    rows = tc.shape[0]
    step = rows // chunks

    pairs = (
        (idx_hbm, idx_ref), (live_hbm, live_ref), (counts_hbm, counts_ref),
        (virt_hbm, virt_ref), (occ_hbm, occ_ref), (tc_hbm, tc),
    )
    loads = [
        pltpu.make_async_copy(src, dst, load_sem.at[i]) for i, (src, dst) in enumerate(pairs)
    ]
    for load in loads:
        load.start()

    barrier = pltpu.get_barrier_semaphore()

    @pl.loop(1, n)
    def _(k):
        pl.semaphore_signal(
            barrier, inc=1, device_id={"aux": lax.rem(me + k, n)}, device_id_type=MESH
        )

    for peer in (twin, across):
        pl.semaphore_signal(barrier, inc=1, device_id={"grp": peer}, device_id_type=MESH)

    mine = pl.multiple_of(core * part, part)

    def stage(a):
        blocks = (virt_ref, virt_ref, occ_ref)[a]
        cols = (slice(0, half), slice(half, 2 * half), slice(None))[a]
        send, stack = sends[a], stacks[a]

        @pl.loop(1, n)
        def _(k):
            t = lax.rem(me + k, n)
            keep = live_ref[0, t].astype(jnp.float32)
            piece = blocks[idx_ref[0, t], pl.ds(mine, part), cols]
            send[t] = (piece.astype(jnp.float32) * keep).astype(jnp.bfloat16)

        keep = live_ref[0, me].astype(jnp.float32)
        own = blocks[idx_ref[0, me], :, cols]
        stack[pl.ds(pl.multiple_of(me * size, size), size), :] = (
            own.astype(jnp.float32) * keep
        ).astype(jnp.bfloat16)

    def out_copy(a, t):
        here = pl.ds(pl.multiple_of(me * size + core * part, part), part)
        return pltpu.make_async_remote_copy(
            sends[a].at[t], stacks[a].at[here, :], send_sem.at[a, t], recv_sem.at[a, me],
            device_id={"aux": t}, device_id_type=MESH,
        )

    def in_copy(a, s):
        there = pl.ds(pl.multiple_of(s * size + core * part, part), part)
        return pltpu.make_async_remote_copy(
            sends[a].at[s], stacks[a].at[there, :], send_sem.at[a, s], recv_sem.at[a, s],
            device_id={"aux": s}, device_id_type=MESH,
        )

    def pass_copy(a, s, side):
        spot = pl.ds(pl.multiple_of(s * size + side * part, part), part)
        return pltpu.make_async_remote_copy(
            stacks[a].at[spot, :], stacks[a].at[spot, :], pass_sem.at[a, s], got_sem.at[a, s],
            device_id={"grp": twin}, device_id_type=MESH,
        )

    def start_all(a):
        @pl.loop(1, n)
        def _(k):
            out_copy(a, lax.rem(me + k, n)).start()

    def sent_all(a):
        @pl.loop(1, n)
        def _(k):
            out_copy(a, lax.rem(me + k, n)).wait_send()

    def pass_all(a):
        @pl.loop(1, n)
        def _(k):
            s = lax.rem(me + n - k, n)
            in_copy(a, s).wait_recv()
            pass_copy(a, s, core).start()

    def got_all(a):
        @pl.loop(1, n)
        def _(k):
            s = lax.rem(me + n - k, n)
            pass_copy(a, s, 1 - core).wait_recv()
            pass_copy(a, s, core).wait_send()

    def product(a, first):
        stack = stacks[a]
        wide = tc.shape[1]
        deep = min(depth, wide)

        def term(i, total):
            at = pl.ds(pl.multiple_of(i * deep, deep), deep)
            return total + jnp.dot(
                tc[first : first + step, at], stack[at, :], preferred_element_type=jnp.float32
            )

        if wide == deep:
            return jnp.dot(
                tc[first : first + step, :], stack[...], preferred_element_type=jnp.float32
            )
        return lax.fori_loop(
            0, wide // deep, term, jnp.zeros((step, stack.shape[1]), jnp.float32)
        )

    def gather_copy(kind, origin, h, j, peer):
        cols = slice(h * half, (h + 1) * half)
        lane = h * chunks + j
        spot = pl.ds(pl.multiple_of(origin * rows + j * step, step), step)
        return pltpu.make_async_remote_copy(
            half_virt.at[spot, cols], half_virt.at[spot, cols], gs_sem.at[kind, lane], gr_sem.at[kind, lane],
            device_id={"grp": peer}, device_id_type=MESH,
        )

    for load in loads[:4]:
        load.wait()
    def half_product(h):
        for j in range(chunks):
            spot = pl.ds(pl.multiple_of(g * rows + j * step, step), step)
            half_virt[spot, h * half : (h + 1) * half] = product(h, j * step).astype(jnp.bfloat16)
            gather_copy(0, g, h, j, across).start()
            gather_copy(1, g, h, j, twin).start()

    def relay(h):
        for j in range(chunks):
            gather_copy(0, across, h, j, across).wait_recv()
            gather_copy(2, across, h, j, twin).start()

    stage(0)
    pl.semaphore_wait(barrier, n + 1)
    start_all(0)
    stage(1)
    loads[4].wait()
    stage(2)
    sent_all(0)
    start_all(1)
    pass_all(0)
    loads[5].wait()
    got_all(0)
    half_product(0)
    sent_all(1)
    start_all(2)
    pass_all(1)
    got_all(1)
    half_product(1)
    relay(0)
    relay(1)
    pass_all(2)
    got_all(2)

    column = lax.broadcasted_iota(jnp.int32, (1, 2 * half), 1)
    owner = column // group_width
    limit = jnp.zeros_like(column)
    for q in range(counts_ref.shape[0]):
        limit = jnp.where(owner == q, counts_ref[q], limit)
    mask = jnp.where(column - owner * group_width < limit, 1.0, 0.0).astype(jnp.float32)
    for j in range(chunks):
        half_occ[j * step : (j + 1) * step, :] = (product(2, j * step) * mask).astype(jnp.bfloat16)

    sent_all(2)
    for h in range(2):
        for j in range(chunks):
            gather_copy(0, g, h, j, across).wait_send()
            gather_copy(1, g, h, j, twin).wait_send()
            gather_copy(1, twin, h, j, twin).wait_recv()
            gather_copy(2, across, h, j, twin).wait_send()
            gather_copy(2, opposite, h, j, twin).wait_recv()


def body(occ_blocks, virt_blocks, three_center, blk_index, blk_live, live_counts):
    n = lax.axis_size("aux")
    parts = lax.axis_size("grp")
    local, size, width = occ_blocks.shape
    rows, slots = three_center.shape
    widths = (width // 2, width // 2, width)
    scale = 1.0 / math.sqrt(width)
    hbm = pl.BlockSpec(memory_space=pltpu.HBM)
    vmem = pl.BlockSpec(memory_space=pltpu.VMEM)
    dma = pltpu.SemaphoreType.DMA
    half_occ, half_virt = pl.pallas_call(
        functools.partial(route, n),
        out_shape=(
            jax.ShapeDtypeStruct((rows, width), jnp.bfloat16),
            jax.ShapeDtypeStruct((parts * rows, width), jnp.bfloat16),
        ),
        in_specs=[hbm] * 6,
        out_specs=(vmem, vmem),
        scratch_shapes=[
            pltpu.SMEM((1, n), jnp.int32),
            pltpu.SMEM((1, n), jnp.int32),
            pltpu.SMEM(live_counts.shape, jnp.int32),
            pltpu.VMEM((local, size, width), jnp.bfloat16),
            pltpu.VMEM((local, size, width), jnp.bfloat16),
            *[pltpu.VMEM((n, size // 2, w), jnp.bfloat16) for w in widths],
            *[pltpu.VMEM((n * size, w), jnp.bfloat16) for w in widths],
            pltpu.VMEM((rows, slots), jnp.bfloat16),
            dma((6,)),
            dma((3, n)), dma((3, n)), dma((3, n)), dma((3, n)),
            dma((3, 2 * chunks)), dma((3, 2 * chunks)),
        ],
        compiler_params=pltpu.CompilerParams(
            collective_id=0, has_side_effects=True, vmem_limit_bytes=48 * 1024 * 1024
        ),
        cost_estimate=pl.CostEstimate(
            flops=4 * rows * slots * width, bytes_accessed=2 * rows * slots, transcendentals=0
        ),
    )(*[
        pltpu.with_memory_space_constraint(x, pltpu.HBM)
        for x in (blk_index.T, blk_live.T, live_counts, occ_blocks, virt_blocks, three_center)
    ])
    return (
        lax.dot_general(
            half_occ, half_virt, (((1,), (1,)), ((), ())), preferred_element_type=jnp.float32
        )
        * scale
    )


def solution(mesh):
    placed = (
        P("aux", None, None),
        P("aux", None, None),
        P(("aux", "grp"), None),
        P(None, "aux"),
        P(None, "aux"),
        P(),
    )
    return jax.shard_map(
        body, mesh=mesh, in_specs=placed, out_specs=P(("aux", "grp"), None), check_vma=False
    )
```
